32 devices in a mesh: dp: 16 (over z, y, x), tensor: 2 (over core).
Axes of the slice: x: 2, y: 2, z: 4, core: 2. Of those that a mesh axis runs over, the one named last changes fastest.
Arguments:
- tokens: bfloat16 [16384, 768], P('dp'), may hold values from -6 to 6
- cotangent: bfloat16 [16384, 768], P('dp'), may hold values from -6 to 6
- group_ids: int32 [16], P('dp'), may hold values from 0 to 15
- group_rows: int32 [16], replicated, may hold values from 64 to 1023
- qkv_master: float32 [768, 3, 768], P('dp', None, 'tensor'), may hold values from -0.21875 to 0.21875
- out_master: float32 [768, 768], P('tensor', 'dp'), may hold values from -1.25 to 1.25
- fc_master: float32 [768, 4, 768], P('dp', None, 'tensor'), may hold values from -0.21875 to 0.21875
- proj_master: float32 [4, 768, 768], P(None, 'tensor', 'dp'), may hold values from -0.109375 to 0.109375
- qkv_moment: float32 [768, 3, 768], P('dp', None, 'tensor'), may hold values from -768 to 768
- out_moment: float32 [768, 768], P('tensor', 'dp'), may hold values from -80 to 80
- fc_moment: float32 [768, 4, 768], P('dp', None, 'tensor'), may hold values from -256 to 256
- proj_moment: float32 [4, 768, 768], P(None, 'tensor', 'dp'), may hold values from -384 to 384
- vectors: float32 [12, 768], replicated, may hold values from -1.2 to 2.2, as said below
- vec_first: float32 [12, 768], replicated, may hold values from -80 to 80
- vec_second: float32 [12, 768], replicated, may hold values from 8.192 to 65.536
Outputs:
- block_out: bfloat16 [16384, 768], P('dp')
- grad_input: bfloat16 [16384, 768], P('dp')
- qkv_new: float32 [768, 3, 768], P('dp', None, 'tensor')
- out_new: float32 [768, 768], P('tensor', 'dp')
- fc_new: float32 [768, 4, 768], P('dp', None, 'tensor')
- proj_new: float32 [4, 768, 768], P(None, 'tensor', 'dp')
- qkv_moment_new: float32 [768, 3, 768], P('dp', None, 'tensor')
- out_moment_new: float32 [768, 768], P('tensor', 'dp')
- fc_moment_new: float32 [768, 4, 768], P('dp', None, 'tensor')
- proj_moment_new: float32 [4, 768, 768], P(None, 'tensor', 'dp')
- qkv_copy: bfloat16 [768, 3, 768], P('dp', None, 'tensor')
- out_copy: bfloat16 [768, 768], P('tensor', 'dp')
- fc_copy: bfloat16 [768, 4, 768], P('dp', None, 'tensor')
- proj_copy: bfloat16 [4, 768, 768], P(None, 'tensor', 'dp')
- vec_first_new: float32 [12, 768], replicated
- vec_second_new: float32 [12, 768], replicated
- vectors_new: float32 [12, 768], replicated
The draws below stay inside these ranges and needn't reach their ends.
Inputs may be any that keep to these rules, and one draw needn't show every extreme that they name: `vectors`: rows 0 and 2 are positive.
All inputs are finite; a program needn't handle non-finite values.
Results may differ from the reference program's by a relative error of at most 0.015.
Values may be sent and summed in bfloat16 or wider, within the bound.
A program may use at most 128 MiB of HBM per device.

```python
import math
import jax
import jax.numpy as jnp
from jax import lax

D = 768
HD = 64
FF = 3072
LEN = 1024
GROUPS = 16
NS_STEPS = 3
ADAM_STEP = 10
SEQS = 16
TOKENS = 16384
VROWS = 12


def draw_vectors(key, part):
    key = jax.random.fold_in(key, 11)
    first_key, second_key = jax.random.split(key)
    line_ids = jnp.arange(VROWS, dtype=jnp.int32)[:, None]
    ramp = 0.6 + 1.2 * jnp.arange(D, dtype=jnp.float32)[None, :] / D
    factor = jax.random.uniform(first_key, (VROWS, D), jnp.float32, 0.85, 1.15)
    offset = jnp.clip(0.3 * jax.random.normal(second_key, (VROWS, D), jnp.float32), -1.2, 1.2)
    gain_rows = (line_ids == 0) | (line_ids == 2)
    return jnp.where(gain_rows, ramp * factor, offset)


def set_ends(entries, rng, smallest, top_value):
    place = [jax.random.randint(jax.random.fold_in(rng, axis), (), 0, length) for axis, length in enumerate(entries.shape)]
    longest = entries.shape.index(max(entries.shape))
    beside = place[:longest] + [(place[longest] + 1) % entries.shape[longest]] + place[longest + 1:]
    return entries.at[tuple(place)].set(smallest).at[tuple(beside)].set(top_value)


def steps_of(own_key, extent, pieces, smallest, top_value):
    def one(dim, shards_of):
        draws = jax.random.uniform(jax.random.fold_in(jax.random.fold_in(own_key, 6), dim), (shards_of,), jnp.float32, smallest / len(pieces), top_value / len(pieces))
        return jnp.repeat(jnp.exp(draws), extent[dim] // shards_of).reshape((-1,) + (1,) * (len(extent) - dim - 1))

    level = one(*pieces[0])
    for cut in pieces[1:]:
        level = level * one(*cut)
    return level


def noise(key, extent, scale, most, cuts=(), held_as=jnp.bfloat16):
    result = jax.random.normal(key, extent, jnp.float32) * scale
    if len(cuts) > 0:
        result = steps_of(key, extent, cuts, -0.22, 0.18) * result
    return jnp.clip(result, min=-most, max=most).astype(held_as)


def setup_inputs(seed: int = 0) -> dict:
    splits = jax.random.split(jax.random.key(seed), 16)
    tokens = noise(splits[0], (TOKENS, D), 1.0, 6.0, ((0, 16),))
    cotangent = noise(splits[1], (TOKENS, D), 1.0, 6.0, ((0, 16),))
    group_ids = set_ends(jax.random.randint(splits[2], (SEQS,), 0, GROUPS), jax.random.fold_in(splits[2], 1), 0, GROUPS - 1).astype(jnp.int32)
    group_rows = set_ends(jax.random.randint(splits[3], (GROUPS,), 64, 1024), jax.random.fold_in(splits[3], 1), 64, 1023).astype(jnp.int32)
    qkv_master = noise(splits[4], (D, 3, D), D ** -0.5, 0.21875, ((0, 16), (2, 2)), jnp.float32)
    out_master = noise(splits[5], (D, D), (D // 32) ** -0.5, 1.25, ((0, 2), (1, 16)), jnp.float32)
    fc_master = noise(splits[6], (D, FF // D, D), D ** -0.5, 0.21875, ((0, 16), (2, 2)), jnp.float32)
    proj_master = noise(splits[7], (FF // D, D, D), FF ** -0.5, 0.109375, ((1, 2), (2, 16)), jnp.float32)
    qkv_moment = noise(splits[8], (D, 3, D), (1.0 * TOKENS ** 0.5), 768.0, ((0, 16), (2, 2)), jnp.float32)
    out_moment = noise(splits[9], (D, D), (0.1 * TOKENS ** 0.5), 80.0, ((0, 2), (1, 16)), jnp.float32)
    fc_moment = noise(splits[10], (D, FF // D, D), (0.35 * TOKENS ** 0.5), 256.0, ((0, 16), (2, 2)), jnp.float32)
    proj_moment = noise(splits[11], (FF // D, D, D), (0.5 * TOKENS ** 0.5), 384.0, ((1, 2), (2, 16)), jnp.float32)
    vectors = draw_vectors(jax.random.fold_in(splits[15], 71), 0)
    vec_first = noise(splits[13], (VROWS, D), (0.11 * TOKENS ** 0.5), 80.0, (), jnp.float32)
    vec_second = jnp.clip(jnp.exp(jax.random.uniform(splits[14], (VROWS, D), jnp.float32, math.log(8.192), math.log(65.536))), 8.192, 65.536)
    return dict(tokens=tokens, cotangent=cotangent, group_ids=group_ids, group_rows=group_rows, qkv_master=qkv_master, out_master=out_master, fc_master=fc_master, proj_master=proj_master, qkv_moment=qkv_moment, out_moment=out_moment, fc_moment=fc_moment, proj_moment=proj_moment, vectors=vectors, vec_first=vec_first, vec_second=vec_second)


HIGH = lax.Precision.HIGHEST
COEF_A = 3.4445
COEF_B = -4.775
COEF_C = 2.0315
MUON_DECAY = 0.5
MUON_RATES = (2.0, 5.0, 2.0, 1.0)
ADAM_RATE = 0.3
BETA_ONE = 0.9
BETA_TWO = 0.999
NORM_EPS = 1e-05

@jax.custom_vjp
def low(v):
    return lax.optimization_barrier(v.astype(jnp.bfloat16)).astype(jnp.float32)

@jax.custom_vjp
def low_back(v):
    return v

def low_keep(v):
    return (low(v), None)

def low_pass(kept, grad):
    return (grad,)

def back_keep(v):
    return (v, None)

def back_low(kept, grad):
    return (low(grad),)
low.defvjp(low_keep, low_pass)
low_back.defvjp(back_keep, back_low)

def matmul(left, right):
    return jnp.dot(left, right, precision=HIGH, preferred_element_type=jnp.float32)

def layer_norm(values, gain, shift):
    centred = values - lax.optimization_barrier(jnp.mean(values, -1, keepdims=True))
    spread = lax.optimization_barrier(jnp.mean(centred * centred, -1, keepdims=True))
    return centred * lax.rsqrt(spread + NORM_EPS) * gain + shift

def attention(queries, key_rows, values):
    block_rows = min(512, LEN)
    col_ids = jnp.arange(LEN, dtype=jnp.int32)[None, :]

    def one_block(block_index):
        row_start = (block_index * block_rows).astype(jnp.int32)
        rows_here = lax.dynamic_slice_in_dim(queries, row_start, block_rows, 0)
        raw_scores = jnp.einsum('qhd,khd->hqk', rows_here, key_rows, precision=HIGH)
        scores = low_back(raw_scores * HD ** (-0.5))
        row_ids = row_start + jnp.arange(block_rows, dtype=jnp.int32)[:, None]
        scores = jnp.where(col_ids <= row_ids, scores, -1e+30)
        row_peak = lax.optimization_barrier(jnp.max(scores, -1, keepdims=True))
        log_totals = row_peak + jnp.log(lax.optimization_barrier(jnp.sum(jnp.exp(scores - row_peak), -1, keepdims=True)))
        weights_low = low(jnp.exp(scores - log_totals))
        return jnp.einsum('hqk,khd->qhd', weights_low, values, precision=HIGH)
    blocks = lax.map(jax.checkpoint(one_block), jnp.arange(LEN // block_rows, dtype=jnp.int32))
    return blocks.reshape(LEN, queries.shape[1] * queries.shape[2])

def block_forward(inputs, qkv_w, out_w, fc_w, proj_w, vectors):
    head_count = D // HD
    multiple = FF // D
    normed_one = low(layer_norm(inputs, vectors[0], vectors[1]))
    qkv_bias = jnp.concatenate([vectors[4], jnp.zeros_like(vectors[4]), vectors[5]])
    projected = low(low_back(matmul(normed_one, qkv_w.reshape(D, 3 * D)) + qkv_bias))
    queries = projected[:, :D].reshape(LEN, head_count, HD)
    key_rows = projected[:, D:2 * D].reshape(LEN, head_count, HD)
    values = projected[:, 2 * D:].reshape(LEN, head_count, HD)
    mixed = low(low_back(attention(queries, key_rows, values)))
    residual = inputs + low_back(matmul(mixed, out_w)) + vectors[6]
    normed_two = low(layer_norm(residual, vectors[2], vectors[3]))
    pre_act = low_back(matmul(normed_two, fc_w.reshape(D, FF)) + vectors[7:7 + multiple].reshape(FF))
    hidden = low(jax.nn.gelu(pre_act, approximate=True))
    return residual + low_back(matmul(hidden, proj_w.reshape(FF, D))) + vectors[7 + multiple]

def orthogonalize(current, tall):
    for sweep_index in range(NS_STEPS):
        if tall:
            gram = low(matmul(current.T, current))
        else:
            gram = low(matmul(current, current.T))
        polynomial = low(COEF_B * gram + COEF_C * matmul(gram, gram))
        if tall:
            product = matmul(current, polynomial)
        else:
            product = matmul(polynomial, current)
        current = low(COEF_A * current + product)
    return current

def reference(tokens, cotangent, group_ids, group_rows, qkv_master, out_master, fc_master, proj_master, qkv_moment, out_moment, fc_moment, proj_moment, vectors, vec_first, vec_second):
    masters = (qkv_master, out_master, fc_master, proj_master)
    weights = tuple((low(master) for master in masters))
    chosen = (group_ids[:, None] == jnp.arange(GROUPS, dtype=jnp.int32)[None, :]).astype(jnp.float32)
    seq_weight = 16.0 * lax.rsqrt(lax.optimization_barrier(jnp.sum(chosen * group_rows.astype(jnp.float32)[None, :], 1)))
    seq_inputs = tokens.astype(jnp.float32).reshape(SEQS, LEN, D)
    seq_cotangents = cotangent.astype(jnp.float32).reshape(SEQS, LEN, D) * seq_weight[:, None, None]
    zero_grads = tuple((jnp.zeros_like(weight) for weight in weights)) + (jnp.zeros_like(vectors),)

    def accumulate(totals_sum, pair):
        seq_in, seq_cot = pair
        seq_out, pullback = jax.vjp(block_forward, seq_in, *weights, vectors)
        gradients = pullback(seq_cot)
        totals_sum = tuple((total + grad for total, grad in zip(totals_sum, gradients[1:])))
        return (totals_sum, (seq_out, gradients[0]))
    gradients, (seq_outs, seq_grads) = lax.scan(accumulate, zero_grads, (seq_inputs, seq_cotangents))
    moments = (qkv_moment, out_moment, fc_moment, proj_moment)
    new_moments = tuple((MUON_DECAY * moment + grad for moment, grad in zip(moments, gradients[:4])))
    flattened = (new_moments[0].reshape(D, 3 * D), new_moments[1], new_moments[2].reshape(D, FF), new_moments[3].reshape(FF, D))
    tall_list = (False, False, False, True)
    new_masters = []
    for matrix_index in range(4):
        matrix = flattened[matrix_index]
        scale = jnp.sqrt(jnp.sum(matrix * matrix))
        start = low(matrix / (scale + 1e-07))
        orthogonal = orthogonalize(start, tall_list[matrix_index])
        master = masters[matrix_index]
        new_masters.append(master - MUON_RATES[matrix_index] * orthogonal.reshape(master.shape))
    vec_grad = gradients[4]
    first_new = BETA_ONE * vec_first + (1.0 - BETA_ONE) * vec_grad
    second_new = BETA_TWO * vec_second + (1.0 - BETA_TWO) * vec_grad * vec_grad
    fix_one = 1.0 - BETA_ONE ** ADAM_STEP
    fix_two = 1.0 - BETA_TWO ** ADAM_STEP
    vectors_new = vectors - ADAM_RATE * (first_new / fix_one) / (jnp.sqrt(second_new / fix_two) + 1e-08)
    return (seq_outs.reshape(TOKENS, D).astype(jnp.bfloat16), seq_grads.reshape(TOKENS, D).astype(jnp.bfloat16), new_masters[0], new_masters[1], new_masters[2], new_masters[3], new_moments[0], new_moments[1], new_moments[2], new_moments[3], new_masters[0].astype(jnp.bfloat16), new_masters[1].astype(jnp.bfloat16), new_masters[2].astype(jnp.bfloat16), new_masters[3].astype(jnp.bfloat16), first_new, second_new, vectors_new)
```

```python
from functools import partial

import jax
import jax.numpy as jnp
from jax import lax
from jax.experimental import pallas as pl
from jax.experimental.pallas import tpu as pltpu
from jax.sharding import PartitionSpec as P

HD = 64
NS_STEPS = 3
ADAM_STEP = 10


COEF_A = 3.4445
COEF_B = -4.775
COEF_C = 2.0315
MUON_DECAY = 0.5
MUON_RATES = (2.0, 5.0, 2.0, 1.0)
ADAM_RATE = 0.3
BETA_ONE = 0.9
BETA_TWO = 0.999
NORM_EPS = 1e-05

BF = jnp.bfloat16
F32 = jnp.float32
MESH = pl.DeviceIdType.MESH
VMEM_LIMIT = 60 * 2**20


def my_place(dims):
    _, y_size, x_size = dims
    me = lax.axis_index("dp")
    return (
        lax.div(me, y_size * x_size),
        lax.rem(lax.div(me, x_size), y_size),
        lax.rem(me, x_size),
    )


def chip_at(dims, z, y, x):
    return (z * dims[1] + y) * dims[2] + x


def hail(peers):
    barrier = pltpu.get_barrier_semaphore()
    for peer in peers:
        pl.semaphore_signal(barrier, inc=1, device_id=peer, device_id_type=MESH)
    return lambda: pl.semaphore_wait(barrier, len(peers))


def remote(src, dst, send, recv, peer):
    return pltpu.make_async_remote_copy(
        src_ref=src, dst_ref=dst, send_sem=send, recv_sem=recv, device_id=peer, device_id_type=MESH
    )


class Gather:
    def __init__(self, dims, chunks, out, ssem, rsem):
        self.dims, self.chunks, self.out = dims, chunks, out
        self.ssem, self.rsem = ssem, rsem
        self.z, self.y, self.x = my_place(dims)

    def peer(self, z, y, x):
        return {"dp": chip_at(self.dims, z, y, x)}

    def peers(self):
        z, y, x = self.z, self.y, self.x
        size = self.dims[0]
        return [self.peer(lax.rem(z + d, size), y, x) for d in range(1, size)] + [
            self.peer(z, y, 1 - x),
            self.peer(z, 1 - y, x),
        ]

    def whole(self, k):
        start, one, two = self.chunks[k]
        return pl.ds(start, one + two)

    def move(self, k, slot, ref, peer):
        return remote(ref, ref, self.ssem.at[k, slot], self.rsem.at[k, slot], peer)

    def along_z(self, k, d):
        z, y, x = self.z, self.y, self.x
        there = self.peer(lax.rem(z + d, self.dims[0]), y, x)
        return self.move(k, d - 1, self.out.at[self.whole(k), z, y, x], there)

    def back_z(self, d):
        return lax.rem(self.z + self.dims[0] - d, self.dims[0])

    def to_x(self, k, d):
        z, y, x = self.z, self.y, self.x
        slot = self.dims[0] - 1 + d
        return self.move(k, slot, self.out.at[self.whole(k), self.back_z(d), y, x], self.peer(z, y, 1 - x))

    def to_y(self, k, d):
        z, y, x = self.z, self.y, self.x
        slot = 2 * self.dims[0] - 1 + d
        return self.move(k, slot, self.out.at[self.whole(k), self.back_z(d), y, x], self.peer(z, 1 - y, x))

    def on_x(self, k):
        z, y, x = self.z, self.y, self.x
        slot = 3 * self.dims[0] - 1
        start, one, _ = self.chunks[k]
        return self.move(k, slot, self.out.at[pl.ds(start, one), :, 1 - y, x], self.peer(z, y, 1 - x))

    def on_y(self, k):
        z, y, x = self.z, self.y, self.x
        slot = 3 * self.dims[0]
        start, one, two = self.chunks[k]
        return self.move(k, slot, self.out.at[pl.ds(start + one, two), :, y, 1 - x], self.peer(z, 1 - y, x))

    def step_one(self, k):
        for d in range(1, self.dims[0]):
            self.along_z(k, d).start()
        self.to_x(k, 0).start()
        self.to_y(k, 0).start()

    def step_two(self, k):
        for d in range(1, self.dims[0]):
            self.along_z(k, d).wait_recv()
            self.to_x(k, d).start()
            self.to_y(k, d).start()

    def step_three(self, k):
        for d in range(self.dims[0]):
            self.to_y(k, d).wait_recv()
        self.on_x(k).start()
        for d in range(self.dims[0]):
            self.to_x(k, d).wait_recv()
        self.on_y(k).start()

    def arrived(self, k):
        self.on_x(k).wait_recv()
        self.on_y(k).wait_recv()

    def finish(self, k):
        for d in range(1, self.dims[0]):
            self.along_z(k, d).wait_send()
        for d in range(self.dims[0]):
            self.to_x(k, d).wait_send()
            self.to_y(k, d).wait_send()
        self.on_x(k).wait_send()
        self.on_y(k).wait_send()


class Scatter:
    def __init__(self, dims, chunks, sources, bufs, lsem, ssem, rsem):
        self.dims, self.sources = dims, sources
        self.rx, self.ry, self.tx, self.ty, self.s, self.rz = bufs
        self.lsem, self.ssem, self.rsem = lsem, ssem, rsem
        self.z, self.y, self.x = my_place(dims)
        self.slot, self.ones, self.twos, self.alls = {}, {}, {}, {}
        one = two = 0
        for n, k in enumerate(sources):
            _, more_one, more_two = chunks[k]
            self.slot[k] = n
            self.ones[k] = pl.ds(one, more_one)
            self.twos[k] = pl.ds(two, more_two)
            self.alls[k] = pl.ds(one + two, more_one + more_two)
            one, two = one + more_one, two + more_two

    peer = Gather.peer
    peers = Gather.peers

    def load_plane(self, k):
        src = self.sources[k][0].at[pl.ds(self.sources[k][1], self.alls[k].size)]
        return pltpu.make_async_copy(src, self.s.at[self.alls[k]], self.lsem.at[self.slot[k]])

    def first(self, k):
        return pl.ds(self.sources[k][1], self.ones[k].size)

    def second(self, k):
        return pl.ds(self.sources[k][1] + self.ones[k].size, self.twos[k].size)

    def xs(self, k, y):
        return self.sources[k][0].at[self.first(k), :, y, self.x]

    def ys(self, k, x):
        return self.sources[k][0].at[self.second(k), :, self.y, x]

    def move(self, k, hop, src, dst, peer):
        i = self.slot[k]
        return remote(src, dst, self.ssem.at[i, hop], self.rsem.at[i, hop], peer)

    def x_one(self, k):
        src = self.sources[k][0].at[self.first(k), :, :, 1 - self.x]
        return self.move(k, 0, src, self.rx.at[self.ones[k]], self.peer(self.z, self.y, 1 - self.x))

    def y_one(self, k):
        src = self.sources[k][0].at[self.second(k), :, 1 - self.y]
        return self.move(k, 1, src, self.ry.at[self.twos[k]], self.peer(self.z, 1 - self.y, self.x))

    def y_two(self, k):
        there = self.peer(self.z, 1 - self.y, self.x)
        return self.move(k, 2, self.xs(k, 1 - self.y), self.tx.at[self.ones[k]], there)

    def x_two(self, k):
        there = self.peer(self.z, self.y, 1 - self.x)
        return self.move(k, 3, self.ys(k, 1 - self.x), self.ty.at[self.twos[k]], there)

    def along_z(self, k, d):
        there = lax.rem(self.z + d, self.dims[0])
        src, dst = self.s.at[self.alls[k], there], self.rz.at[self.alls[k], d - 1]
        return self.move(k, 3 + d, src, dst, self.peer(there, self.y, self.x))

    def step_one(self, k):
        self.x_one(k).start()
        self.y_one(k).start()

    def step_two(self, k):
        self.x_one(k).wait_recv()
        for y in (1 - self.y, self.y):
            mine = self.xs(k, y)
            mine[...] = mine[...] + self.rx[self.ones[k], :, y]
        self.y_two(k).start()
        self.y_one(k).wait_recv()
        for x in (1 - self.x, self.x):
            mine = self.ys(k, x)
            mine[...] = mine[...] + self.ry[self.twos[k], :, x]
        self.x_two(k).start()

    def plane_sums(self, k):
        start, size = self.alls[k].start, self.ones[k].size
        self.y_two(k).wait_recv()
        self.s[pl.ds(start, size)] = self.xs(k, self.y)[...] + self.tx[self.ones[k]]
        self.x_two(k).wait_recv()
        self.s[pl.ds(start + size, self.twos[k].size)] = self.ys(k, self.x)[...] + self.ty[self.twos[k]]

    def step_three(self, k):
        if self.sources[k][2] == PLANE:
            self.load_plane(k).wait()
        else:
            self.plane_sums(k)
        for d in range(1, self.dims[0]):
            self.along_z(k, d).start()

    def total(self, k):
        for d in range(1, self.dims[0]):
            self.along_z(k, d).wait_recv()
        value = self.s[self.alls[k], self.z].astype(F32)
        for d in range(1, self.dims[0]):
            value = value + self.rz[self.alls[k], d - 1].astype(F32)
        return [beside(value, n, 3) for n in range(0, self.alls[k].size, 3)]

    def finish_plane(self, k):
        for copy in (self.x_one(k), self.y_one(k), self.y_two(k), self.x_two(k)):
            copy.wait_send()

    def finish_z(self, k):
        for d in range(1, self.dims[0]):
            self.along_z(k, d).wait_send()


IN_PLACE, PLANE = range(2)


def beside(value, first, count):
    return jnp.concatenate([value[first + n] for n in range(count)], 1)


def put_beside(array, first, index, value):
    lanes = array.shape[-1]
    for n in range(value.shape[1] // lanes):
        part = value[:, n * lanes : (n + 1) * lanes]
        array[(first + n, *index)] = part


def scatter_scratch(dims, rows, chunks, sources):
    z, y, x = dims
    lanes = 2 * HD
    one = sum(chunks[k][1] for k in sources)
    two = sum(chunks[k][2] for k in sources)
    dma = pltpu.SemaphoreType.DMA
    return [
        pltpu.VMEM((one, z, y, rows, lanes), BF),
        pltpu.VMEM((two, z, x, rows, lanes), BF),
        pltpu.VMEM((one, z, rows, lanes), BF),
        pltpu.VMEM((two, z, rows, lanes), BF),
        pltpu.VMEM((one + two, z, rows, lanes), BF),
        pltpu.VMEM((one + two, z - 1, rows, lanes), BF),
        dma((len(sources),)),
        dma((len(sources), z + 3)),
        dma((len(sources), z + 3)),
    ]


class VectorSum:
    def __init__(self, dims, vec, out, held, got, fan, ssem, rsem):
        self.dims, self.vec, self.out, self.held, self.got, self.fan = dims, vec, out, held, got, fan
        self.ssem, self.rsem = ssem, rsem
        self.z, self.y, self.x = my_place(dims)
        self.t = lax.axis_index("tensor")

    peer = Gather.peer

    def hop(self, i):
        z, y, x = self.z, self.y, self.x
        src = self.vec if i == 0 else self.held.at[i - 1]
        peer = ({"tensor": 1 - self.t}, self.peer(z, y, 1 - x), self.peer(z, 1 - y, x))[i]
        return remote(src, self.got.at[i], self.ssem.at[i], self.rsem.at[i], peer)

    def along_z(self, d):
        z, y, x = self.z, self.y, self.x
        return remote(
            self.held.at[2],
            self.fan.at[z],
            self.ssem.at[2 + d],
            self.rsem.at[2 + d],
            self.peer(lax.rem(z + d, self.dims[0]), y, x),
        )

    def step(self, i):
        if i == 0:
            self.hop(0).start()
        elif i <= 3:
            self.hop(i - 1).wait_recv()
            before = self.vec[...] if i == 1 else self.held[i - 2]
            self.held[i - 1] = before + self.got[i - 1]
            if i < 3:
                self.hop(i).start()
            else:
                for d in range(1, self.dims[0]):
                    self.along_z(d).start()
                self.fan[self.z] = self.held[2]
        elif i == 4:
            for d in range(1, self.dims[0]):
                self.along_z(d).wait_recv()
            value = self.fan[0]
            for z in range(1, self.dims[0]):
                value = value + self.fan[z]
            self.out[...] = value
            for j in range(3):
                self.hop(j).wait_send()
            for d in range(1, self.dims[0]):
                self.along_z(d).wait_send()


def vector_scratch(dims, shape):
    return [
        pltpu.VMEM((3, *shape), F32),
        pltpu.VMEM((3, *shape), F32),
        pltpu.VMEM((dims[0], *shape), F32),
        pltpu.SemaphoreType.DMA((2 + dims[0],)),
        pltpu.SemaphoreType.DMA((2 + dims[0],)),
    ]


class Pair:
    def __init__(self, ssem, rsem):
        self.ssem, self.rsem = ssem, rsem
        self.other = {"tensor": 1 - lax.axis_index("tensor")}

    def send(self, i, src, dst):
        return remote(src, dst, self.ssem.at[i], self.rsem.at[i], self.other)


def dot(left, right, dims, kind=F32):
    return lax.dot_general(left, right, (dims, ((), ())), preferred_element_type=kind)


NN = ((1,), (0,))
NT = ((1,), (1,))
TN = ((0,), (0,))


def adam(vec_grad, vectors, vec_first, vec_second):
    first_new = BETA_ONE * vec_first + (1.0 - BETA_ONE) * vec_grad
    second_new = BETA_TWO * vec_second + (1.0 - BETA_TWO) * vec_grad * vec_grad
    fix_one = 1.0 - BETA_ONE**ADAM_STEP
    fix_two = 1.0 - BETA_TWO**ADAM_STEP
    vectors_new = vectors - ADAM_RATE * (first_new / fix_one) / (jnp.sqrt(second_new / fix_two) + 1e-08)
    return first_new, second_new, vectors_new


PLANE_OF_QKV = 1
QKV_OWNED = (0, 2, 3)


def owner_of(b):
    if b < FIRST_FC:
        return PLANE_OF_QKV, b // 2, b % 2
    r, odd = divmod(b - FIRST_FC, 2)
    return (2 if odd else 0), r // 2, r % 2


class Muon:
    def __init__(self, dims, bufs, sems, pair):
        self.dims, self.pair = dims, pair
        self.sent, self.block, self.acc, self.low, self.got = bufs[:5]
        self.quarters, self.near, self.summed, self.both, self.exact, self.work, self.poly, self.factor, self.come = bufs[5:]
        self.a_ssem, self.a_rsem, self.o_ssem, self.o_rsem, self.p_ssem, self.p_rsem = sems
        self.z, self.y, self.x = my_place(dims)
        self.me = lax.axis_index("dp")
        self.t = lax.axis_index("tensor")
        self.spot = 2 * self.y + self.x
        self.owns = self.z < 3
        self.late = self.z == PLANE_OF_QKV
        self.early = (self.z == 0) | (self.z == 2)
        self.chips = dims[0] * dims[1] * dims[2]
        self.size = TILE
        odd = lax.rem(self.z, 2)
        self.mine = (1 - odd) * (FIRST_FC + 2 * self.spot + lax.div(self.z, 2)) + odd * self.spot

    def pieces(self, b):
        if b >= FIRST_FC or b == OUT_BLOCK:
            whole = pl.ds(0, self.sent.shape[2])
            return [(0, b, whole, whole)]
        lanes = 2 * HD
        there = pl.ds(PAIR_BLOCKS.index(b) * lanes, lanes)
        return [(n, QKV_OWNED[n], pl.ds(n * lanes, lanes), there) for n in range(3)]

    def give(self, b, piece):
        n, owned, here, there = piece
        src = self.sent.at[b, :, here]
        dst = self.block.at[self.z, self.y, self.x, :, there]
        sem = self.a_rsem.at[self.me, there.start // there.size]
        return remote(src, dst, self.a_ssem.at[b, n], sem, {"dp": chip_at(self.dims, *owner_of(owned))})

    def share(self, b, value):
        self.sent[b] = value
        for piece in self.pieces(b):
            _, owned, here, there = piece
            owner = chip_at(self.dims, *owner_of(owned))

            @pl.when(self.me != owner)
            def _():
                self.give(b, piece).start()

            @pl.when(self.me == owner)
            def _():
                self.block[self.z, self.y, self.x, :, there] = self.sent[b, :, here]

    def other(self, d):
        return lax.rem(self.me + d, self.chips)

    def wait_for(self, places):
        @pl.loop(1, self.chips)
        def _(d):
            src = self.other(d)
            y_size, x_size = self.dims[1:]
            z, y, x = lax.div(src, y_size * x_size), lax.rem(lax.div(src, x_size), y_size), lax.rem(src, x_size)
            for n, there in enumerate(places):
                dst = self.block.at[z, y, x, :, there]
                copy = remote(self.sent.at[0, :, there], dst, self.a_ssem.at[0, 0], self.a_rsem.at[src, n], {"dp": src})
                copy.wait_recv()

    def gram(self):
        lanes, alone = 2 * HD, (self.spot == 1) | (self.z != PLANE_OF_QKV)

        @pl.when(alone)
        def _():
            self.wait_for([pl.ds(0, self.sent.shape[2])])

        @pl.when(~alone)
        def _():
            self.wait_for([pl.ds(p * lanes, lanes) for p in range(3)])

        value = self.block[...]
        value = value.reshape(-1, value.shape[-1])
        size = self.size
        for h, tiles in enumerate(GRAM_HALVES):
            for n, (row, column) in enumerate(tiles):
                left = value[row * size : (row + 1) * size]
                tile = dot(left, value[column * size : (column + 1) * size], NT)
                self.acc[h, n] = tile
                self.low[h, n] = tile.astype(BF)
        self.to_core().start()

    def to_core(self):
        return self.pair.send(0, self.low.at[1 - self.t], self.got)

    def plane(self, i, src, dst, y, x):
        there = {"dp": chip_at(self.dims, self.z, y, x)}
        return remote(src, dst, self.p_ssem.at[i], self.p_rsem.at[i], there)

    def around(self):
        y, x = self.y, self.x
        return ((y, 1 - x), (1 - y, x), (1 - y, 1 - x))

    def to_sum(self, n):
        y, x = self.around()[n]
        return self.plane(n, self.quarters.at[2 * y + x], self.near.at[n], y, x)

    def to_all(self, n):
        y, x = self.around()[n]
        return self.plane(3 + n, self.summed.at[self.spot], self.summed.at[self.spot], y, x)

    def across_cores(self):
        self.to_core().wait_recv()
        part = self.size // 4
        for n in range(len(GRAM_HALVES[0])):
            value = (self.acc[self.t, n] + self.got[n].astype(F32)).astype(BF)
            for q in range(4):
                self.quarters[q, n] = value[q * part : (q + 1) * part]
        for n in (2, 0, 1):
            self.to_sum(n).start()

    def alone(self, spot):
        return (self.z == PLANE_OF_QKV) & (spot == 1)

    def across_plane(self):
        total = jnp.where(self.alone(self.spot), 0.0, self.quarters[self.spot].astype(F32))
        for n, (y, x) in enumerate(self.around()):
            self.to_sum(n).wait_recv()
            total = total + jnp.where(self.alone(2 * y + x), 0.0, self.near[n].astype(F32))
        self.summed[self.spot] = total.astype(BF)
        for n in (2, 0, 1):
            self.to_all(n).start()

    def to_both(self):
        return self.pair.send(1, self.both.at[self.t], self.both.at[self.t])

    def gather_plane(self):
        for n in range(3):
            self.to_all(n).wait_recv()
        self.both[self.t] = jnp.where(self.alone(self.spot), self.quarters[...], self.summed[...])
        self.to_both().start()

    def begin(self):
        self.to_both().wait_recv()
        size = self.size
        norm = jnp.zeros((1, 1), F32)
        tiles = {}
        for h, places in enumerate(GRAM_HALVES):
            for n, (row, column) in enumerate(places):
                tile = jnp.concatenate([self.both[h, q, n] for q in range(4)], 0).astype(F32)
                if row == column:
                    down = lax.broadcasted_iota(jnp.int32, tile.shape, 0)
                    across = lax.broadcasted_iota(jnp.int32, tile.shape, 1)
                    norm = norm + jnp.sum(jnp.where(down == across, tile, 0.0), keepdims=True)
                tiles[row, column] = tile
        self.scale = 1.0 / (jnp.sqrt(norm) + 1e-07)
        square = self.scale * self.scale
        for (row, column), tile in tiles.items():
            tile = tile * square
            places = [(row, column, tile)] + ([(column, row, tile.T)] if row != column else [])
            for down, across, part in places:
                here = (slice(down * size, (down + 1) * size), slice(across * size, (across + 1) * size))
                self.exact[here] = part
                self.work[(0, *here)] = part.astype(BF)

    def polynomial(self, sweep):
        low = self.work[sweep % 2]
        self.poly[...] = (COEF_B * self.exact[...] + COEF_C * dot(low, low, NN)).astype(BF)

    def advance(self, sweep):
        low, poly = self.work[sweep % 2], self.poly[...]
        size = low.shape[0] // 2
        for i in range(2):
            here = pl.ds(i * size, size)
            left = COEF_A * self.exact[here, :] + dot(self.poly[here, :], low, NN)
            value = COEF_A * left + dot(left.astype(BF), poly, NN)
            self.exact[here, :] = value
            self.work[(sweep + 1) % 2, here, :] = value.astype(BF)

    def apply(self, sweep):
        if sweep == 0:
            value = self.block[...]
            value = value.reshape(-1, value.shape[-1])
        else:
            value = self.factor[(sweep - 1) % 2]
        if sweep < NS_STEPS - 1:
            rows = COEF_A * value.astype(F32) + dot(self.poly[...], value, NN)
        else:
            low = self.work[sweep % 2]
            inner = COEF_B * value.astype(F32) + COEF_C * dot(low, value, NN)
            rows = self.scale * (COEF_A * value.astype(F32) + dot(low, inner.astype(BF), NN))
        self.factor[sweep % 2] = rows.astype(BF)

    def orthogonalize(self):
        self.begin()
        for sweep in range(NS_STEPS - 1):
            self.polynomial(sweep)
            self.apply(sweep)
            self.advance(sweep)
        self.apply(NS_STEPS - 1)

    def rows_for(self, chip):
        count = self.come.shape[1]
        return self.factor.at[(NS_STEPS - 1) % 2, pl.ds(pl.multiple_of(chip * count, 16), count), :]

    def back(self, there):
        return remote(
            self.rows_for(there), self.come.at[self.mine], self.o_ssem.at[there], self.o_rsem.at[self.mine], {"dp": there}
        )

    def hand_back(self):
        @pl.loop(0, self.chips)
        def _(i):
            there = self.chips - 1 - i

            @pl.when(there != self.me)
            def _():
                self.back(there).start()

        self.come[self.mine] = self.rows_for(self.me)[...]

    def result(self, b):
        there = chip_at(self.dims, *owner_of(b))

        @pl.when(self.me != there)
        def _():
            remote(
                self.rows_for(there), self.come.at[b], self.o_ssem.at[0], self.o_rsem.at[b], {"dp": there}
            ).wait_recv()

        return self.come[b].astype(F32)

    def finish(self):
        for b in range(self.come.shape[0]):

            for piece in self.pieces(b):

                @pl.when(self.me != chip_at(self.dims, *owner_of(piece[1])))
                def _():
                    self.give(b, piece).wait_send()

        @pl.when(self.owns)
        def _():
            self.to_core().wait_send()
            self.to_both().wait_send()
            for n in range(3):
                self.to_sum(n).wait_send()
                self.to_all(n).wait_send()

            @pl.loop(0, self.chips)
            def _(there):
                @pl.when(there != self.me)
                def _():
                    self.back(there).wait_send()


GRAM_HALVES = (((0, 0), (1, 0), (2, 0)), ((1, 1), (2, 1), (2, 2)))


def muon_scratch(dims, count, rows, local, width):
    chips = dims[0] * dims[1] * dims[2]
    part = TILE // 4
    dma = pltpu.SemaphoreType.DMA
    return [
        pltpu.VMEM((count, rows, local), BF),
        pltpu.VMEM((*dims, rows, local), BF),
        pltpu.VMEM((2, 3, TILE, TILE), F32),
        pltpu.VMEM((2, 3, TILE, TILE), BF),
        pltpu.VMEM((3, TILE, TILE), BF),
        pltpu.VMEM((4, 3, part, TILE), BF),
        pltpu.VMEM((3, 3, part, TILE), BF),
        pltpu.VMEM((4, 3, part, TILE), BF),
        pltpu.VMEM((2, 4, 3, part, TILE), BF),
        pltpu.VMEM((width, width), F32),
        pltpu.VMEM((2, width, width), BF),
        pltpu.VMEM((width, width), BF),
        pltpu.VMEM((2, width, local), BF),
        pltpu.VMEM((count, rows, local), BF),
        dma((count, 3)),
        dma((chips, 3)),
        dma((chips,)),
        dma((count,)),
        dma((6,)),
        dma((6,)),
    ]


TILE = 256


def pair_columns(p):
    return [lanes_at(3 * p + n) for n in range(3)]


def lanes_at(n, count=1):
    lanes = 2 * HD
    return pl.ds(n * lanes if isinstance(n, int) else pl.multiple_of(n * lanes, lanes), count * lanes)


def first_of_pair(p):
    return 3 * (p + lax.div(p + 1, 2))


def head_masks():
    lane = lax.broadcasted_iota(jnp.int32, (TILE, 2 * HD), 1)
    return [jnp.where(lane < HD, 1.0, 0.0).astype(BF), jnp.where(lane < HD, 0.0, 1.0).astype(BF)]


def causal(value, other):
    key_ids = lax.broadcasted_iota(jnp.int32, value.shape, 0)
    query_ids = lax.broadcasted_iota(jnp.int32, value.shape, 1)
    return jnp.where(key_ids <= query_ids, value, other)


def key_pieces(i):
    pieces = [(i * TILE, TILE, True)]
    start = 0
    while start < i * TILE:
        size = min(2 * TILE, i * TILE - start)
        pieces.append((start, size, False))
        start += size
    return pieces


def key_rows(i):
    return TILE * i * (i + 1) // 2


class AttentionForward:
    def __init__(self, qkv, mixed, values_t, probs, probs_out, sems):
        self.qkv, self.mixed, self.values_t = qkv, mixed, values_t
        self.probs, self.probs_out, self.sems = probs, probs_out, sems
        self.length = mixed.shape[0]

    def keep(self, p):
        return pltpu.make_async_copy(self.probs.at[lax.rem(p, 2)], self.probs_out.at[p], self.sems.at[p])

    def pair(self, p):
        q_cols, k_cols, v_cols = pair_columns(p)
        masks = head_masks()
        slot = lax.rem(p, 2)

        @pl.when(p >= 2)
        def _():
            self.keep(p - 2).wait()

        self.values_t[...] = self.qkv[:, v_cols].T
        for i in range(self.length // TILE):
            here = pl.ds(i * TILE, TILE)
            query = self.qkv[here, q_cols] * jnp.bfloat16(HD**-0.5)
            found = []
            for h in range(2):
                scores = []
                for start, size, diagonal in key_pieces(i):
                    score = dot(self.qkv[pl.ds(start, size), k_cols], query * masks[h], NT)
                    scores.append(causal(score, -1e30) if diagonal else score)
                peak = jnp.max(scores[0], 0, keepdims=True)
                for score in scores[1:]:
                    peak = jnp.maximum(peak, jnp.max(score, 0, keepdims=True))
                probs = [jnp.exp(score - peak) for score in scores]
                share = 1.0 / sum(jnp.sum(prob, 0, keepdims=True) for prob in probs)
                out = 0.0
                for (start, size, _), prob in zip(key_pieces(i), probs):
                    low = (prob * share).astype(BF)
                    self.probs[slot, h, pl.ds(key_rows(i) + start, size), :] = low
                    out = out + dot(self.values_t[h * HD : (h + 1) * HD, pl.ds(start, size)], low, NN)
                found.append(out)
            self.mixed[here, lanes_at(p)] = jnp.concatenate(found, 0).T.astype(BF)
        self.keep(p).start()


PAIR_BLOCKS = (0, 2, 3)
OUT_BLOCK = 1
FIRST_FC = 4


def block_of(arrays, b):
    qkv, out, fc, proj = arrays
    lanes = 2 * HD
    if b == OUT_BLOCK:
        return out[...]
    if b < FIRST_FC:
        p = PAIR_BLOCKS.index(b)
        return jnp.concatenate([qkv[n, :, p * lanes : (p + 1) * lanes] for n in range(3)], 1)
    r, odd = divmod(b - FIRST_FC, 2)
    return proj[r] if odd else fc[:, r, :]


def put_block(arrays, b, value):
    qkv, out, fc, proj = arrays
    lanes = 2 * HD
    if b == OUT_BLOCK:
        out[...] = value
    elif b < FIRST_FC:
        p = PAIR_BLOCKS.index(b)
        for n in range(3):
            qkv[n, :, p * lanes : (p + 1) * lanes] = value[:, n * lanes : (n + 1) * lanes]
    else:
        r, odd = divmod(b - FIRST_FC, 2)
        if odd:
            proj[r] = value
        else:
            fc[:, r, :] = value


def matrix_of(b):
    return 1 if b == OUT_BLOCK else 0 if b < FIRST_FC else 2 + (b - FIRST_FC) % 2


FRONT_CHUNKS = ((0, 2, 1), (6, 1, 2), (9, 2, 1), (3, 1, 2), (12, 3, 3), (18, 3, 3), (24, 3, 3), (30, 3, 3))
FRONT_EARLY = (4, 5)
BACK_CHUNKS = ((0, 3, 3), (6, 1, 2), (9, 2, 1), (12, 3, 3), (18, 3, 3), (24, 3, 3), (30, 3, 3))
BACK_ORDER = (5, 6, 0, 1, 2, 3, 4)


def front_kernel(dims, *refs):
    masters = refs[:4]
    group_ids, group_rows, vectors, tokens_in, cotangent_in = refs[4:9]
    vec, block_out_far, resid_low_far, ready_out, halfway_out = refs[9:14]
    mixed_out, qkv_out, normed_t_out, weights_out, probs_out = refs[14:19]
    scratch = list(refs[19:])

    def take(count):
        taken = scratch[:count]
        del scratch[:count]
        return taken

    tokens, cotangent, block_out, resid_low, ready = take(5)
    mixed, qkv, normed_t = take(3)
    full, normed, normed_two, normed_two_t, top_low, top_t, hidden, grad_pre = take(8)
    part_sum, sent, got, values_t, made, probs = take(6)
    in_sem, out_sem, tile_sem, probs_sem = take(4)
    loads = [
        pltpu.make_async_copy(src, dst, in_sem.at[i])
        for i, (src, dst) in enumerate(((tokens_in, tokens), (cotangent_in, cotangent)))
    ]
    for load in loads:
        load.start()
    g = Gather(dims, FRONT_CHUNKS, full, *take(2))
    pair = Pair(*take(2))
    sources = {k: (made, 6 * n, IN_PLACE) for n, k in enumerate(FRONT_EARLY)}
    s = Scatter(dims, FRONT_CHUNKS, sources, take(6), *take(3))
    attention = AttentionForward(qkv, mixed, values_t, probs, probs_out, probs_sem)
    length, width = tokens.shape
    local = mixed.shape[1]
    blocks = length // TILE
    count = len(FRONT_CHUNKS)
    start_here = lax.axis_index("tensor") * local
    place = pl.ds(pl.multiple_of(start_here, 128), local)

    def pack(k):
        start, one, two = FRONT_CHUNKS[k]
        for b in range(start // 3, (start + one + two) // 3):
            put_beside(full, 3 * b, (g.z, g.y, g.x), block_of(masters, b).astype(BF))

    keeping = []

    def keep(src, dst):
        copy = pltpu.make_async_copy(src, dst, out_sem.at[len(keeping)])
        copy.start()
        keeping.append(copy)

    def weight(b):
        return jnp.concatenate([full[3 * b + n].reshape(width, 2 * HD) for n in range(3)], 1)

    def rows_of(i):
        return pl.ds(pl.multiple_of(i * TILE, TILE), TILE)

    def two_of(i):
        return pl.ds(pl.multiple_of(i * 2 * TILE, 2 * TILE), 2 * TILE)

    def swap(n, i):
        here = rows_of(i)
        return pair.send(n * blocks + i, sent.at[n, here, :], got.at[n, here, :])

    def both(n, here):
        return sent[n, here, :].astype(F32) + got[n, here, :].astype(F32)

    def unit_of(values):
        centred = values - jnp.mean(values, -1, keepdims=True)
        root = lax.rsqrt(jnp.mean(centred * centred, -1, keepdims=True) + NORM_EPS)
        return centred * root, root

    def residual(here):
        return tokens[here, :].astype(F32) + both(0, here) + vectors[6:7, :]

    everyone_is_here = hail(g.peers() + [pair.other])
    pack(0)
    everyone_is_here()
    g.step_one(0)
    for k in range(1, count - 1):
        pack(k)
        g.step_one(k)
    pack(count - 1)
    vec[...] = jnp.zeros_like(vec)
    loads[0].wait()

    @pl.loop(0, blocks)
    def _(i):
        here = rows_of(i)
        unit, _ = unit_of(tokens[here, :].astype(F32))
        low = (unit * vectors[0:1, :] + vectors[1:2, :]).astype(BF)
        normed[here, :] = low
        normed_t[:, here] = low.T

    chosen = lax.broadcasted_iota(jnp.int32, group_rows.shape, 1) == group_ids[...]
    rows_here = jnp.sum(jnp.where(chosen, group_rows[...].astype(F32), 0.0), keepdims=True)
    seq_weight = 16.0 * lax.rsqrt(rows_here)

    keep(normed_t, normed_t_out)
    g.step_two(0)
    g.step_three(0)
    g.step_two(1)
    g.step_three(1)
    g.step_two(2)
    loads[1].wait()

    @pl.loop(0, blocks)
    def _(i):
        here = rows_of(i)
        grad_top = cotangent[here, :].astype(F32) * seq_weight
        low = grad_top.astype(BF)
        top_low[here, :] = low
        top_t[:, here] = low.T
        vec[11:12, :] += 0.5 * jnp.sum(grad_top, 0, keepdims=True)

    def project(p):
        lanes = 2 * HD
        here_p = pl.ds(pl.multiple_of(start_here + p * lanes, 128), lanes)
        zeros = jnp.zeros((1, lanes), F32)
        bias = jnp.concatenate([vectors[4:5, here_p], zeros, vectors[5:6, here_p]], 1)

        @pl.loop(0, blocks // 2)
        def _(i):
            here = two_of(i)
            weights = [full[first_of_pair(p) + n].reshape(width, lanes) for n in range(3)]
            value = dot(normed[here, :], jnp.concatenate(weights, 1), NN) + bias
            qkv[here, lanes_at(3 * p, 3)] = value.astype(BF)

    g.step_three(2)
    g.step_two(3)
    g.step_two(4)
    g.step_one(7)

    @pl.loop(0, 3)
    def _(p):
        for k in range(3):
            pl.when(p == k)(partial(g.arrived, k))
        project(p)

        @pl.when(p == 1)
        def _():
            g.step_three(3)
            g.step_two(5)

        @pl.when(p == 2)
        def _():
            g.step_three(4)

        attention.pair(p)

    g.step_three(5)
    keep(mixed, mixed_out)
    keep(qkv, qkv_out)
    g.arrived(3)
    keep(full.at[pl.ds(0, 3 * FIRST_FC)], weights_out)

    @pl.loop(0, blocks)
    def _(i):
        here = rows_of(i)
        sent[0, here, :] = dot(mixed[here, :], weight(OUT_BLOCK), NT).astype(BF)
        swap(0, i).start()

    g.step_two(6)
    g.step_two(7)

    @pl.loop(0, blocks)
    def _(i):
        here = rows_of(i)
        swap(0, i).wait_recv()
        unit, _ = unit_of(residual(here))
        low = (unit * vectors[2:3, :] + vectors[3:4, :]).astype(BF)
        normed_two[here, :] = low
        normed_two_t[:, here] = low.T

    root_two = 0.7978845608028654

    def feed_forward(r, last, i):
        here = two_of(i)
        fc, proj = FIRST_FC + 2 * r, FIRST_FC + 1 + 2 * r
        value = dot(normed_two[here, :], weight(fc), NN) + vectors[7 + r : 8 + r, place]
        square = value * value
        bent = jnp.tanh(root_two * (value + 0.044715 * (square * value)))
        unit = (0.5 * value * (1.0 + bent)).astype(BF)
        slope = 0.5 * (1.0 + bent) + (0.5 * root_two) * value * (1.0 - bent * bent) * (1.0 + (3 * 0.044715) * square)
        hidden[here, :] = unit
        back = (dot(top_low[here, :], weight(proj), NN) * slope).astype(BF)
        grad_pre[here, :] = back
        vec[7 + r : 8 + r, place] += jnp.sum(back.astype(F32), 0, keepdims=True)
        out = dot(unit, weight(proj), NT)
        grad = dot(back, weight(fc), NT)
        if r > 0:
            out = out + part_sum[0, here, :]
            grad = grad + part_sum[1, here, :]
        if last:
            sent[1, here, :] = out.astype(BF)
            sent[2, here, :] = grad.astype(BF)
            for n in range(2):
                swap(2, 2 * i + n).start()
                swap(1, 2 * i + n).start()
        else:
            part_sum[0, here, :] = out
            part_sum[1, here, :] = grad

    def weight_gradient(left, right, into, b):
        parts = 2
        z = dims[0] // parts
        size = width // parts
        for part in range(parts):
            value = dot(left[part * size : (part + 1) * size, :], right[...], NN).astype(BF)
            for n in range(3):
                block = value[:, n * 2 * HD : (n + 1) * 2 * HD]
                into[3 * b + n, part * z : (part + 1) * z] = block.reshape(z, *into.shape[2:])

    def forth(r):
        g.arrived(4 + r)
        pl.loop(0, blocks // 2)(partial(feed_forward, r, r == 3))

    def back(into, b):
        weight_gradient(normed_two_t, grad_pre, into, b)
        weight_gradient(top_t, hidden, into, b + 1)

    first, second = FRONT_EARLY
    forth(0)
    g.step_three(6)
    back(made, 0)
    s.step_one(first)
    forth(1)
    back(made, 2)
    g.step_three(7)
    forth(2)
    s.step_one(second)
    back(ready, 0)
    s.step_two(first)
    forth(3)
    back(ready, 2)
    keep(ready, ready_out)
    s.step_two(second)

    def tile_out(n, i):
        here = rows_of(i)
        src, dst = ((block_out, block_out_far), (resid_low, resid_low_far))[n]
        return pltpu.make_async_copy(src.at[here, :], dst.at[here, :], tile_sem.at[n, i])

    @pl.loop(0, blocks)
    def _(i):
        here = rows_of(i)
        swap(1, i).wait_recv()
        value = residual(here)
        block_out[here, :] = (value + both(1, here) + vectors[11:12, :]).astype(BF)
        tile_out(0, i).start()
        swap(2, i).wait_recv()
        grad = both(2, here)
        unit, root = unit_of(value)
        scaled = grad * vectors[2:3, :]
        inner = jnp.mean(scaled * unit, -1, keepdims=True)
        grad_top = cotangent[here, :].astype(F32) * seq_weight
        total = grad_top + root * (scaled - jnp.mean(scaled, -1, keepdims=True) - unit * inner)
        resid_low[here, :] = total.astype(BF)
        tile_out(1, i).start()
        vec[2:3, :] += 0.5 * jnp.sum(grad * unit, 0, keepdims=True)
        vec[3:4, :] += 0.5 * jnp.sum(grad, 0, keepdims=True)
        vec[6:7, :] += 0.5 * jnp.sum(total, 0, keepdims=True)

    for n, k in enumerate(FRONT_EARLY):
        s.plane_sums(k)
        keep(s.s.at[s.alls[k]], halfway_out.at[pl.ds(6 * n, 6)])
    for k in range(count):
        g.finish(k)
    for k in FRONT_EARLY:
        s.finish_plane(k)
    for copy in keeping:
        copy.wait()
    for p in (1, 2):
        attention.keep(jnp.int32(p)).wait()

    @pl.loop(0, blocks)
    def _(i):
        for n in range(2):
            tile_out(n, i).wait()
        for n in range(3):
            swap(n, i).wait_send()


def forward_mlp(dims, masters, tokens, cotangent, group_ids, group_rows, vectors, collective_id):
    rows, local = masters[1].shape
    count = 4 + 2 * masters[3].shape[0]
    length, width = tokens.shape
    blocks = length // TILE
    vmem = pl.BlockSpec(memory_space=pltpu.VMEM)
    hbm = pl.BlockSpec(memory_space=pl.ANY)
    dma = pltpu.SemaphoreType.DMA
    lanes = 2 * HD
    hops = 3 * dims[0] + 1
    return pl.pallas_call(
        partial(front_kernel, dims),
        out_shape=(
            jax.ShapeDtypeStruct(vectors.shape, F32),
            jax.ShapeDtypeStruct(tokens.shape, BF),
            jax.ShapeDtypeStruct(tokens.shape, BF),
            jax.ShapeDtypeStruct((12, *dims, rows, lanes), BF),
            jax.ShapeDtypeStruct((12, dims[0], rows, lanes), BF),
            jax.ShapeDtypeStruct((length, local), BF),
            jax.ShapeDtypeStruct((length, 3 * local), BF),
            jax.ShapeDtypeStruct((width, length), BF),
            jax.ShapeDtypeStruct((3 * FIRST_FC, *dims, rows, lanes), BF),
            jax.ShapeDtypeStruct((3, 2, key_rows(blocks), TILE), BF),
        ),
        in_specs=[vmem] * 7 + [hbm] * 2,
        out_specs=(vmem,) + (hbm,) * 9,
        scratch_shapes=[
            pltpu.VMEM(tokens.shape, BF),
            pltpu.VMEM(tokens.shape, BF),
            pltpu.VMEM(tokens.shape, BF),
            pltpu.VMEM(tokens.shape, BF),
            pltpu.VMEM((12, *dims, rows, lanes), BF),
            pltpu.VMEM((length, local), BF),
            pltpu.VMEM((length, 3 * local), BF),
            pltpu.VMEM((width, length), BF),
            pltpu.VMEM((3 * count, *dims, rows, lanes), BF),
            pltpu.VMEM(tokens.shape, BF),
            pltpu.VMEM(tokens.shape, BF),
            pltpu.VMEM((width, length), BF),
            pltpu.VMEM(tokens.shape, BF),
            pltpu.VMEM((width, length), BF),
            pltpu.VMEM((length, local), BF),
            pltpu.VMEM((length, local), BF),
            pltpu.VMEM((2, *tokens.shape), F32),
            pltpu.VMEM((3, *tokens.shape), BF),
            pltpu.VMEM((3, *tokens.shape), BF),
            pltpu.VMEM((lanes, length), BF),
            pltpu.VMEM((12, *dims, rows, lanes), BF),
            pltpu.VMEM((2, 2, key_rows(blocks), TILE), BF),
            dma((2,)),
            dma((7,)),
            dma((2, blocks)),
            dma((3,)),
            dma((len(FRONT_CHUNKS), hops)),
            dma((len(FRONT_CHUNKS), hops)),
            dma((3 * blocks,)),
            dma((3 * blocks,)),
        ]
        + scatter_scratch(dims, rows, FRONT_CHUNKS, FRONT_EARLY),
        compiler_params=pltpu.CompilerParams(
            collective_id=collective_id, has_side_effects=True, vmem_limit_bytes=VMEM_LIMIT
        ),
        name="forward_mlp",
    )(*masters, group_ids.reshape(1, 1), group_rows.reshape(1, -1), vectors, tokens, cotangent)


class AttentionBack:
    def __init__(self, qkv, probs, mixed, grad_mixed, grad_qkv, key_sum, value_sum, keys_t):
        self.qkv, self.probs, self.mixed, self.grad_mixed, self.grad_qkv = qkv, probs, mixed, grad_mixed, grad_qkv
        self.key_sum, self.value_sum, self.keys_t = key_sum, value_sum, keys_t
        self.length = mixed.shape[0]

    def pair(self, p):
        lanes = 2 * HD
        q_cols, k_cols, v_cols = pair_columns(p)
        m_cols = lanes_at(p)
        masks = head_masks()
        self.keys_t[...] = self.qkv[:, k_cols].T
        for i in range(self.length // TILE):
            here = pl.ds(i * TILE, TILE)
            query = self.qkv[here, q_cols] * jnp.bfloat16(HD**-0.5)
            grad = self.grad_mixed[here, m_cols]
            each = (grad.astype(F32) * self.mixed[here, m_cols].astype(F32)).T
            deltas = [jnp.sum(each[h * HD : (h + 1) * HD], 0, keepdims=True) for h in range(2)]
            queries = [query * mask for mask in masks]
            grads = [grad * mask for mask in masks]
            queries_low = jnp.concatenate(queries, 0)
            grads_low = jnp.concatenate(grads, 0)
            found = [0.0, 0.0]
            for start, size, diagonal in key_pieces(i):
                there = pl.ds(start, size)
                values = self.qkv[there, v_cols]
                probs, scores = [], []
                for h in range(2):
                    prob = self.probs[p, h, pl.ds(key_rows(i) + start, size), :]
                    probs.append(prob)
                    scores.append((prob.astype(F32) * (dot(values, grads[h], NT) - deltas[h])).astype(BF))
                value_part = dot(jnp.concatenate(probs, 1), grads_low, NN)
                key_part = dot(jnp.concatenate(scores, 1), queries_low, NN)
                if diagonal:
                    self.value_sum[there, :] = value_part
                    self.key_sum[there, :] = key_part
                else:
                    self.value_sum[there, :] += value_part
                    self.key_sum[there, :] += key_part
                for h in range(2):
                    found[h] = found[h] + dot(self.keys_t[h * HD : (h + 1) * HD, there], scores[h], NN)
            self.grad_qkv[here, q_cols] = (jnp.concatenate(found, 0) * HD**-0.5).T.astype(BF)
        self.grad_qkv[:, k_cols] = self.key_sum[...].astype(BF)
        self.grad_qkv[:, v_cols] = self.value_sum[...].astype(BF)


def back_kernel(dims, *refs):
    vec_in, vectors = refs[:2]
    ready, halfway, far = refs[2], refs[3], refs[4:15]
    grad_input_out, moments_out, steps, vec_sum = refs[15:19]
    scratch = list(refs[19:])

    def take(count):
        taken = scratch[:count]
        del scratch[:count]
        return taken

    near = take(11)
    in_sem, out_sem, grad_input, moments_new = take(4)
    pieces = [(far[0].at[p], near[0].at[p]) for p in range(3)] + list(zip(far[1:], near[1:]))
    loads = [pltpu.make_async_copy(src, dst, in_sem.at[i]) for i, (src, dst) in enumerate(pieces)]
    probs, weights, resid_low, mixed, qkv, normed_t, tokens = near[:7]
    moments = near[7:]
    load_probs, load_acts, load_moments = loads[:3], loads[3:9], loads[9:]
    made, grad_mixed, grad_qkv, gh_sent, gh_got = take(5)
    sources = {5: (made, 12, IN_PLACE), 6: (made, 18, IN_PLACE)}
    load_ready = [
        pltpu.make_async_copy(ready.at[pl.ds(6 * n, 6)], made.at[pl.ds(12 + 6 * n, 6)], out_sem.at[2 + n])
        for n in range(2)
    ]
    sources.update({k: (made, BACK_CHUNKS[k][0], IN_PLACE) for k in (0, 1, 2)})
    sources.update({3: (halfway, 0, PLANE), 4: (halfway, 6, PLANE)})
    s = Scatter(dims, BACK_CHUNKS, sources, take(6), *take(3))
    (vec,) = take(1)
    v = VectorSum(dims, vec, vec_sum, *take(5))
    pair = Pair(*take(2))
    m = Muon(dims, take(14), take(6), pair)
    attention = AttentionBack(qkv, probs, mixed, grad_mixed, grad_qkv, *take(3))
    everyone_is_here = hail([{"dp": m.other(d)} for d in range(1, m.chips)] + [pair.other])
    length, width = tokens.shape
    local = mixed.shape[1]
    blocks = length // TILE
    pairs = local // (2 * HD)
    def sums(k):
        start, one, two = BACK_CHUNKS[k]
        for n, total in enumerate(s.total(k)):
            b = start // 3 + n
            value = MUON_DECAY * block_of(moments, b) + total
            moments_new[b] = value
            m.share(b, value.astype(BF))

    keeping = []

    def keep(src, dst):
        copy = pltpu.make_async_copy(src, dst, out_sem.at[len(keeping)])
        copy.start()
        keeping.append(copy)

    def rows_of(i):
        return pl.ds(pl.multiple_of(i * TILE, TILE), TILE)

    def weight(b):
        return jnp.concatenate([weights[3 * b + n].reshape(width, 2 * HD) for n in range(3)], 1)

    def into_made(first, left, right):
        parts = 2
        z = dims[0] // parts
        size = width // parts
        for part in range(parts):
            value = dot(left[part * size : (part + 1) * size, :], right, NN).astype(BF)
            for n in range(3):
                block = value[:, n * 2 * HD : (n + 1) * 2 * HD]
                made[first + n, part * z : (part + 1) * z] = block.reshape(z, *made.shape[2:])

    def pair_gradient(p):
        into_made(first_of_pair(p), normed_t, grad_qkv[:, lanes_at(3 * p, 3)])

    def send_h(i):
        here = rows_of(i)
        return pair.send(2 + i, gh_sent.at[here, :], gh_got.at[here, :])

    def input_gradient(i):
        here = rows_of(i)
        parts = [dot(grad_qkv[here, p * local : (p + 1) * local], weight(PAIR_BLOCKS[p]), NT) for p in range(pairs)]
        gh_sent[here, :] = sum(parts).astype(BF)
        send_h(i).start()

    def first_norm(i):
        here = rows_of(i)
        send_h(i).wait_recv()
        grad = gh_sent[here, :].astype(F32) + gh_got[here, :].astype(F32)
        values = tokens[here, :].astype(F32)
        centred = values - jnp.mean(values, -1, keepdims=True)
        root = lax.rsqrt(jnp.mean(centred * centred, -1, keepdims=True) + NORM_EPS)
        unit = centred * root
        scaled = grad * vectors[0:1, :]
        inner = jnp.mean(scaled * unit, -1, keepdims=True)
        back = root * (scaled - jnp.mean(scaled, -1, keepdims=True) - unit * inner)
        grad_input[here, :] = (resid_low[here, :].astype(F32) + back).astype(BF)
        vec[0:1, :] += 0.5 * jnp.sum(grad * unit, 0, keepdims=True)
        vec[1:2, :] += 0.5 * jnp.sum(grad, 0, keepdims=True)

    def bias_sums():
        lanes = 2 * HD
        for p in range(pairs):
            place = pl.ds(pl.multiple_of(m.t * local + p * lanes, 128), lanes)
            for row, cols in zip((4, 5), pair_columns(p)[::2]):
                vec[row : row + 1, place] += jnp.sum(grad_qkv[:, cols].astype(F32), 0, keepdims=True)

    vec[...] = vec_in[...]
    for load in load_ready:
        load.start()
    for k in (3, 4):
        s.load_plane(k).start()
    load_ready[0].wait()
    everyone_is_here()
    s.step_one(5)
    for load in load_acts[:4] + load_probs[:1] + load_acts[4:5] + load_moments + load_probs[1:] + load_acts[5:]:
        load.start()
    for load in load_acts[:2]:
        load.wait()

    @pl.loop(0, blocks)
    def _(i):
        here = rows_of(i)
        grad_mixed[here, :] = dot(resid_low[here, :], weight(OUT_BLOCK), NN).astype(BF)

    s.step_three(3)
    load_acts[2].wait()
    into_made(3 * OUT_BLOCK, resid_low[...].T, mixed[...])
    load_ready[1].wait()
    s.step_one(6)
    for load in load_acts[3:5]:
        load.wait()

    def before_gradient(p):
        @pl.when(p == 0)
        def _():
            s.step_two(5)
            s.step_three(4)

        @pl.when(p == 1)
        def _():
            s.step_three(5)
            s.step_three(6)

        @pl.when(p == 2)
        def _():
            s.step_two(1)

    def after_gradient(p):
        @pl.when(p == 0)
        def _():
            s.step_two(6)
            s.step_one(0)

        @pl.when(p == 1)
        def _():
            for load in load_moments:
                load.wait()
            sums(3)
            sums(4)
            s.step_two(0)
            s.step_one(1)

        @pl.when(p == 2)
        def _():
            s.step_three(0)
            s.step_one(2)

    @pl.loop(0, 3)
    def _(p):
        pltpu.make_async_copy(far[0].at[p], near[0].at[p], in_sem.at[p]).wait()
        attention.pair(p)
        before_gradient(p)
        pair_gradient(p)
        after_gradient(p)

    sums(5)
    sums(6)
    pl.loop(0, blocks)(input_gradient)
    s.step_three(1)
    s.step_two(2)
    early, late = pl.when(m.early), pl.when(m.late)

    load_acts[5].wait()
    bias_sums()
    pl.loop(0, blocks // 2)(first_norm)
    s.step_three(2)
    early(m.gram)
    sums(0)
    sums(1)
    pl.loop(blocks // 2, blocks)(first_norm)
    early(m.across_cores)
    sums(2)
    v.step(0)
    keep(grad_input, grad_input_out)
    keep(moments_new, moments_out)
    late(m.gram)
    early(m.across_plane)
    v.step(1)
    late(m.across_cores)
    early(m.gather_plane)
    v.step(2)
    late(m.across_plane)
    v.step(3)
    late(m.gather_plane)

    @pl.when(m.owns)
    def _():
        m.orthogonalize()
        m.hand_back()

    v.step(4)
    for b in range(steps.shape[0]):
        steps[b] = MUON_RATES[matrix_of(b)] * m.result(b)
    for k in sources:
        if sources[k][2] != PLANE:
            s.finish_plane(k)
        s.finish_z(k)
    for copy in keeping:
        copy.wait()

    @pl.loop(0, blocks)
    def _(i):
        send_h(i).wait_send()

    m.finish()


def backward_tail(dims, ready, halfway, acts, vec, moments, vectors, collective_id):
    probs, weights, resid_low, mixed, qkv, normed_t, tokens = acts
    rows, local = moments[1].shape
    count = FIRST_FC + 2 * moments[3].shape[0]
    length, width = tokens.shape
    blocks = length // TILE
    lanes = 2 * HD
    vmem = pl.BlockSpec(memory_space=pltpu.VMEM)
    hbm = pl.BlockSpec(memory_space=pl.ANY)
    wide = jax.ShapeDtypeStruct((count, rows, local), F32)
    dma = pltpu.SemaphoreType.DMA
    far = (probs, weights, resid_low, mixed, qkv, normed_t, tokens, *moments)
    return pl.pallas_call(
        partial(back_kernel, dims),
        out_shape=(jax.ShapeDtypeStruct(tokens.shape, BF), wide, wide, jax.ShapeDtypeStruct(vec.shape, F32)),
        in_specs=[vmem] * 2 + [hbm] * 13,
        out_specs=(hbm,) * 2 + (vmem,) * 2,
        scratch_shapes=[pltpu.VMEM(array.shape, array.dtype) for array in far]
        + [
            dma((len(far) + 2,)),
            dma((4,)),
            pltpu.VMEM(tokens.shape, BF),
            pltpu.VMEM((count, rows, local), F32),
            pltpu.VMEM((24, *dims, rows, lanes), BF),
            pltpu.VMEM(mixed.shape, BF),
            pltpu.VMEM(qkv.shape, BF),
            pltpu.VMEM(tokens.shape, BF),
            pltpu.VMEM(tokens.shape, BF),
        ]
        + scatter_scratch(dims, rows, BACK_CHUNKS, BACK_ORDER)
        + [pltpu.VMEM(vec.shape, F32)]
        + vector_scratch(dims, vec.shape)
        + [dma((2 + blocks,))] * 2
        + muon_scratch(dims, count, rows, local, width)
        + [
            pltpu.VMEM((length, lanes), F32),
            pltpu.VMEM((length, lanes), F32),
            pltpu.VMEM((lanes, length), BF),
        ],
        compiler_params=pltpu.CompilerParams(
            collective_id=collective_id, has_side_effects=True, vmem_limit_bytes=VMEM_LIMIT
        ),
        name="backward_tail",
    )(vec, vectors, ready, halfway, *far)


def finish_kernel(*refs):
    masters = refs[:4]
    moments, steps, block_in, grad_in, vec_sum, vectors, vec_first, vec_second = refs[4:12]
    block_out, grad_out = refs[12:14]
    news, moments_new, copies = refs[14:18], refs[18:22], refs[22:26]
    first_new, second_new, vectors_new = refs[26:]
    block_out[...] = block_in[...]
    grad_out[...] = grad_in[...]
    for b in range(steps.shape[0]):
        put_block(moments_new, b, moments[b])
        if b in QKV_OWNED:
            n = QKV_OWNED.index(b)
            value = masters[0][n] - steps[b]
            news[0][n] = value
            copies[0][n] = value.astype(BF)
        else:
            value = block_of(masters, b) - steps[b]
            put_block(news, b, value)
            put_block(copies, b, value.astype(BF))
    first_new[...], second_new[...], vectors_new[...] = adam(
        vec_sum[...], vectors[...], vec_first[...], vec_second[...]
    )


def finish_step(masters, moments, steps, block_out, grad_input, vec_sum, vectors, vec_first, vec_second):
    vmem = pl.BlockSpec(memory_space=pltpu.VMEM)
    activation = jax.ShapeDtypeStruct(block_out.shape, BF)
    wide = [jax.ShapeDtypeStruct(master.shape, F32) for master in masters]
    narrow = [jax.ShapeDtypeStruct(master.shape, BF) for master in masters]
    small = [jax.ShapeDtypeStruct(vectors.shape, F32)] * 3
    return pl.pallas_call(
        finish_kernel,
        out_shape=(activation, activation, *wide, *wide, *narrow, *small),
        in_specs=[vmem] * 12,
        out_specs=(vmem,) * 17,
        compiler_params=pltpu.CompilerParams(vmem_limit_bytes=VMEM_LIMIT),
        name="finish_step",
    )(*masters, moments, steps, block_out, grad_input, vec_sum, vectors, vec_first, vec_second)


def plain_tail(edges, part, vec, moments, masters, vectors, vec_first, vec_second):
    rows = moments.shape[0]
    width = part.shape[0]
    moments = MUON_DECAY * moments + lax.psum_scatter(part.astype(F32), "dp", scatter_dimension=0, tiled=True)
    full = lax.all_gather(moments.astype(BF), "dp", axis=0, tiled=True)
    start = rows * lax.axis_index("dp")
    eye = jnp.arange(width, dtype=jnp.int32)[None, :] == start + jnp.arange(rows, dtype=jnp.int32)[:, None]
    masters_new = []
    for i in range(4):
        half = full[:, edges[i] : edges[i + 1]]
        gram = lax.psum(dot(half, half, NT), "tensor")
        scale = 1.0 / (jnp.sqrt(jnp.trace(gram)) + 1e-07)
        gram = gram * (scale * scale)
        factors = []
        for sweep in range(NS_STEPS):
            low = gram.astype(BF)
            factors.append((COEF_B * low.astype(F32) + COEF_C * dot(low, low, NN)).astype(BF))
            left = COEF_A * low.astype(F32) + dot(factors[-1], low, NN)
            gram = COEF_A * left + dot(left.astype(BF), factors[-1], NN)
        product = COEF_A * eye + lax.dynamic_slice_in_dim(factors.pop(), start, rows, 0).astype(F32)
        while factors:
            product = COEF_A * product + dot(product.astype(BF), factors.pop(), NN)
        ortho = dot((product * scale).astype(BF), half, NN)
        masters_new.append(masters[:, edges[i] : edges[i + 1]] - MUON_RATES[i] * ortho)
    masters_new = jnp.concatenate(masters_new, 1)
    vec_grad = lax.psum(vec, ("dp", "tensor"))
    return (moments, masters_new, masters_new.astype(BF), *adam(vec_grad, vectors, vec_first, vec_second))


def layer_norm(values, gain, shift):
    centred = values - jnp.mean(values, -1, keepdims=True)
    spread = jnp.mean(centred * centred, -1, keepdims=True)
    return centred * lax.rsqrt(spread + NORM_EPS) * gain + shift


def gelu_tanh(values):
    return jax.nn.gelu(values, approximate=True)


def masked_scores(queries, key_rows, row_start):
    raw_scores = jnp.einsum(
        "qhd,khd->hqk", queries, key_rows, preferred_element_type=jnp.float32
    ) * HD ** (-0.5)
    row_ids = row_start + jnp.arange(queries.shape[0], dtype=jnp.int32)[:, None]
    col_ids = jnp.arange(key_rows.shape[0], dtype=jnp.int32)[None, :]
    return jnp.where(col_ids <= row_ids, raw_scores, -1e30)


def attend_forward(queries, key_rows, values):
    length = queries.shape[0]
    block_rows = min(512, length)
    outputs = []
    totals = []
    for row_start in range(0, length, block_rows):
        row_stop = row_start + block_rows
        scores = masked_scores(queries[row_start:row_stop], key_rows[:row_stop], row_start)
        row_peak = jnp.max(scores, -1, keepdims=True)
        log_totals = row_peak + jnp.log(jnp.sum(jnp.exp(scores - row_peak), -1, keepdims=True))
        weights_low = jnp.exp(scores - log_totals).astype(jnp.bfloat16)
        outputs.append(
            jnp.einsum(
                "hqk,khd->qhd", weights_low, values[:row_stop], preferred_element_type=jnp.float32
            )
        )
        totals.append(log_totals)
    return (jnp.concatenate(outputs, 0), totals)


def attend_backward(queries, key_rows, values, grad_rows, totals):
    length = queries.shape[0]
    block_rows = min(512, length)
    grad_queries = []
    grad_keys = jnp.zeros(key_rows.shape, jnp.float32)
    grad_values = jnp.zeros(values.shape, jnp.float32)
    for block_index, row_start in enumerate(range(0, length, block_rows)):
        row_stop = row_start + block_rows
        rows_here = queries[row_start:row_stop]
        scores = masked_scores(rows_here, key_rows[:row_stop], row_start)
        probs = jnp.exp(scores - totals[block_index])
        probs_low = probs.astype(jnp.bfloat16)
        grad_here = grad_rows[row_start:row_stop]
        grad_values = grad_values.at[:row_stop].add(
            jnp.einsum("hqk,qhd->khd", probs_low, grad_here, preferred_element_type=jnp.float32)
        )
        grad_probs = jnp.einsum(
            "qhd,khd->hqk", grad_here, values[:row_stop], preferred_element_type=jnp.float32
        )
        grad_scores = (
            probs * (grad_probs - jnp.sum(grad_probs * probs, -1, keepdims=True))
        ).astype(jnp.bfloat16)
        grad_queries.append(
            HD ** (-0.5)
            * jnp.einsum(
                "hqk,khd->qhd", grad_scores, key_rows[:row_stop], preferred_element_type=jnp.float32
            )
        )
        grad_keys = grad_keys.at[:row_stop].add(
            HD ** (-0.5)
            * jnp.einsum("hqk,qhd->khd", grad_scores, rows_here, preferred_element_type=jnp.float32)
        )
    return (jnp.concatenate(grad_queries, 0), grad_keys, grad_values)


def plain_layer(
    edges,
    weights,
    tokens,
    cotangent,
    group_ids,
    group_rows,
    moments_old,
    masters,
    vectors,
    vec_first,
    vec_second,
):
    local_width = edges[2] - edges[1]
    multiple = (edges[3] - edges[2]) // local_width
    head_count = local_width // HD
    seq_count = group_ids.shape[0]
    row_total, model_width = tokens.shape
    length = row_total // seq_count
    col_start = lax.axis_index("tensor") * local_width
    qkv_mat, out_t, fc_mat, proj_t = (weights[:, edges[i] : edges[i + 1]] for i in range(4))

    query_bias = lax.dynamic_slice_in_dim(vectors[4], col_start, local_width, 0)
    value_bias = lax.dynamic_slice_in_dim(vectors[5], col_start, local_width, 0)
    fc_bias = lax.dynamic_slice_in_dim(vectors[7 : 7 + multiple], col_start, local_width, 1).reshape(
        multiple * local_width
    )
    inputs = tokens.astype(jnp.float32)
    normed_one = layer_norm(inputs, vectors[0], vectors[1]).astype(jnp.bfloat16)
    qkv_bias = jnp.concatenate([query_bias, jnp.zeros_like(query_bias), value_bias])
    projected = (dot(normed_one, qkv_mat, NN) + qkv_bias).astype(jnp.bfloat16)
    shaped = projected.reshape(seq_count, length, 3, head_count, HD)
    forward = [attend_forward(shaped[s, :, 0], shaped[s, :, 1], shaped[s, :, 2]) for s in range(seq_count)]
    mixed = jnp.concatenate([f[0] for f in forward], 0).reshape(row_total, local_width).astype(jnp.bfloat16)

    def pair_sum(part):
        return lax.psum(part.astype(BF), "tensor").astype(F32)

    attn_out = pair_sum(dot(mixed, out_t, NT))
    residual = inputs + attn_out + vectors[6]
    normed_two = layer_norm(residual, vectors[2], vectors[3]).astype(jnp.bfloat16)
    pre_act = dot(normed_two, fc_mat, NN) + fc_bias
    hidden = gelu_tanh(pre_act).astype(jnp.bfloat16)
    mlp_out = pair_sum(dot(hidden, proj_t, NT))
    block_out = (residual + mlp_out + vectors[7 + multiple]).astype(jnp.bfloat16)
    chosen = (group_ids[:, None] == jnp.arange(group_rows.shape[0], dtype=jnp.int32)[None, :]).astype(jnp.float32)
    seq_weight = 16.0 * lax.rsqrt(jnp.sum(chosen * group_rows.astype(jnp.float32)[None, :], 1))
    grad_top = (
        cotangent.astype(jnp.float32).reshape(seq_count, length, model_width) * seq_weight[:, None, None]
    ).reshape(row_total, model_width)
    top_low = grad_top.astype(jnp.bfloat16)
    grad_proj_t = dot(top_low, hidden, TN).astype(BF)
    grad_hidden = dot(top_low, proj_t, NN)
    grad_pre = jax.vjp(gelu_tanh, pre_act)[1](grad_hidden)[0].astype(jnp.bfloat16)
    grad_fc = dot(normed_two, grad_pre, TN).astype(BF)
    grad_fc_bias = jnp.sum(grad_pre.astype(jnp.float32), 0)
    grad_h_two = pair_sum(dot(grad_pre, fc_mat, NT))
    pull_two = jax.vjp(layer_norm, residual, vectors[2], vectors[3])[1]
    grad_resid_norm, grad_gain_two, grad_shift_two = pull_two(grad_h_two)
    grad_residual = grad_top + grad_resid_norm
    resid_low = grad_residual.astype(jnp.bfloat16)
    def placed(piece):
        filled = jnp.zeros((piece.shape[0], model_width), jnp.float32)
        return lax.dynamic_update_slice_in_dim(filled, piece, col_start, 1)

    nothing = jnp.zeros((2, model_width), jnp.float32)
    vec_local = jnp.concatenate(
        [
            nothing,
            0.5 * jnp.stack([grad_gain_two, grad_shift_two]),
            nothing,
            0.5 * jnp.sum(grad_residual, 0)[None, :],
            placed(grad_fc_bias.reshape(multiple, local_width)),
            0.5 * jnp.sum(grad_top, 0)[None, :],
        ],
        0,
    )
    ready = jnp.concatenate([grad_fc, grad_proj_t], 1)
    rest = (moments_old, masters, vectors, vec_first, vec_second)
    grad_out_t = dot(resid_low, mixed, TN).astype(BF)
    grad_mixed = dot(resid_low, out_t, NN).astype(jnp.bfloat16).reshape(seq_count, length, head_count, HD)
    grad_parts = jnp.concatenate(
        [
            jnp.stack(
                attend_backward(shaped[s, :, 0], shaped[s, :, 1], shaped[s, :, 2], grad_mixed[s], forward[s][1]), 1
            )
            for s in range(seq_count)
        ],
        0,
    )
    grad_qkv = grad_parts.reshape(row_total, 3 * local_width).astype(jnp.bfloat16)
    grad_qkv_w = dot(normed_one, grad_qkv, TN).astype(BF)
    bias_sums = jnp.sum(grad_qkv.astype(jnp.float32), 0)
    grad_h_one = pair_sum(dot(grad_qkv, qkv_mat, NT))
    pull_one = jax.vjp(layer_norm, inputs, vectors[0], vectors[1])[1]
    grad_in_norm, grad_gain_one, grad_shift_one = pull_one(grad_h_one)
    grad_input = (grad_residual + grad_in_norm).astype(jnp.bfloat16)
    vec_local = vec_local.at[:2].add(0.5 * jnp.stack([grad_gain_one, grad_shift_one]))
    vec_local = vec_local.at[4:6].add(
        placed(jnp.stack([bias_sums[:local_width], bias_sums[2 * local_width :]]))
    )
    part = jnp.concatenate([grad_qkv_w, grad_out_t, ready], 1)
    return (block_out, grad_input, *plain_tail(edges, part, vec_local, *rest))


def on_device(
    dims,
    tokens,
    cotangent,
    group_ids,
    group_rows,
    qkv_master,
    out_master,
    fc_master,
    proj_master,
    qkv_moment,
    out_moment,
    fc_moment,
    proj_moment,
    vectors,
    vec_first,
    vec_second,
):
    rows = qkv_master.shape[0]
    local_width = out_master.shape[0]
    multiple = fc_master.shape[1]
    if group_ids.shape[0] != 1 or rows % 16 or tokens.shape[0] % TILE or (local_width, multiple) != (6 * HD, 4):
        dims = None
    widths = (3 * local_width, local_width, multiple * local_width, multiple * local_width)
    edges = [sum(widths[:i]) for i in range(5)]

    def pack(qkv, out, fc, proj):
        return jnp.concatenate(
            [
                qkv.reshape(rows, widths[0]),
                out.T,
                fc.reshape(rows, widths[2]),
                proj.reshape(widths[3], rows).T,
            ],
            1,
        )

    def unpack(packed):
        qkv, out, fc, proj = (packed[:, edges[i] : edges[i + 1]] for i in range(4))
        return (
            qkv.reshape(rows, 3, local_width),
            out.T,
            fc.reshape(rows, multiple, local_width),
            proj.T.reshape(multiple, local_width, rows),
        )

    if dims is not None:

        def views(qkv, out, fc, proj):
            return qkv.transpose(1, 0, 2), out.T, fc, proj.transpose(0, 2, 1)

        masters = views(qkv_master, out_master, fc_master, proj_master)
        moments_old = views(qkv_moment, out_moment, fc_moment, proj_moment)
        vec, block_out, resid_low, ready, halfway, mixed, projected, normed_t, weights, probs = forward_mlp(
            dims, masters, tokens, cotangent, group_ids, group_rows, vectors, 0
        )
        acts = (probs, weights, resid_low, mixed, projected, normed_t, tokens)
        grad_input, moments, steps, vec_sum = backward_tail(
            dims, ready, halfway, acts, vec, moments_old, vectors, 1
        )
        results = finish_step(
            masters, moments, steps, block_out, grad_input, vec_sum, vectors, vec_first, vec_second
        )
        return (*results[:2], *views(*results[2:6]), *views(*results[6:10]), *views(*results[10:14]), *results[14:])
    masters = pack(qkv_master, out_master, fc_master, proj_master)
    moments_old = pack(qkv_moment, out_moment, fc_moment, proj_moment)
    block_out, grad_input, moments, masters_new, copies, *small = plain_layer(
        edges,
        lax.all_gather(masters.astype(BF), "dp", axis=0, tiled=True),
        tokens,
        cotangent,
        group_ids,
        group_rows,
        moments_old,
        masters,
        vectors,
        vec_first,
        vec_second,
    )
    return (block_out, grad_input, *unpack(masters_new), *unpack(moments), *unpack(copies), *small)


def chip_grid(mesh):
    chips = [device.coords for device in mesh.devices[:, 0]]
    x, y, z = (max(chip[axis] for chip in chips) - min(chip[axis] for chip in chips) + 1 for axis in range(3))
    return (z, y, x) if (z, y, x) == (4, 2, 2) and len(chips) == 16 else None


def solution(mesh):
    placed = (
        P("dp", None),
        P("dp", None),
        P("dp"),
        P(),
        P("dp", None, "tensor"),
        P("tensor", "dp"),
        P("dp", None, "tensor"),
        P(None, "tensor", "dp"),
        P("dp", None, "tensor"),
        P("tensor", "dp"),
        P("dp", None, "tensor"),
        P(None, "tensor", "dp"),
        P(),
        P(),
        P(),
    )
    return jax.shard_map(
        partial(on_device, chip_grid(mesh)),
        mesh=mesh,
        in_specs=placed,
        out_specs=(
            P("dp", None),
            P("dp", None),
            P("dp", None, "tensor"),
            P("tensor", "dp"),
            P("dp", None, "tensor"),
            P(None, "tensor", "dp"),
            P("dp", None, "tensor"),
            P("tensor", "dp"),
            P("dp", None, "tensor"),
            P(None, "tensor", "dp"),
            P("dp", None, "tensor"),
            P("tensor", "dp"),
            P("dp", None, "tensor"),
            P(None, "tensor", "dp"),
            P(),
            P(),
            P(),
        ),
        check_vma=False,
    )
```
